256 devices in a mesh: section: 8 (over x, core), tm: 32 (over y, z).
Axes of the slice: x: 4, y: 4, z: 8, core: 2. Of those that a mesh axis runs over, the one named last changes fastest.
Arguments:
- frames: bfloat16 [4, 4096, 2048], P(None, 'tm'), may hold values from -6 to 6
- norm_gain: bfloat16 [8, 2048], P('section'), may hold values from 0.5 to 1.5
- w_qkv: bfloat16 [8, 2048, 3072], P('section', 'tm'), may hold values from -8 to 8
- w_out: bfloat16 [8, 1024, 2048], P('section', 'tm'), may hold values from -0.1875 to 0.1875
- lengths: int32 [4, 1], replicated, may hold values from 1365 to 4096, as said below
- windows: int32 [8], replicated, may hold values from 32 to 64, as said below
- shifts: int32 [8], replicated, may hold values from 0 to 63, as said below
Outputs:
- hidden: bfloat16 [8, 4, 4096, 2048], P('section', None, 'tm')
The draws below stay inside these ranges and needn't reach their ends.
Inputs may be any that keep to these rules, and one draw needn't show every extreme that they name: `lengths`: some micro-batch fills all 4096 frames of its slot. `windows`: some layer has a window of exactly 64. `shifts`: each below its layer's window; some layer shifts by 0 and some by 64 - 1.
All inputs are finite; a program needn't handle non-finite values.
Results may differ from the reference program's by a relative error of at most 0.024.
Values may be sent and summed in bfloat16 or wider, within the bound.
A program may use at most 64 MiB of HBM per device.

```python
import math
import jax
import jax.numpy as jnp
from jax import lax

D = 2048
HEADS = 8
HDIM = 128
FR_DEV = 128
WMAX = 64
MICRO = 4
LAYERS = 8
UTT = 1
CAP = 4096
FRAMES = 4096


def window_plan(key):
    first, second, third, fourth = jax.random.split(key, 4)
    layer_ids = jnp.arange(LAYERS, dtype=jnp.int32)
    window = jax.random.randint(first, (LAYERS,), WMAX // 2, WMAX + 1, dtype=jnp.int32)
    widest = jax.random.randint(second, (), 0, LAYERS, dtype=jnp.int32)
    other = (widest + 1 + jax.random.randint(third, (), 0, LAYERS - 1, dtype=jnp.int32)) % LAYERS
    window = jnp.where(layer_ids == widest, WMAX, window)
    offset = jax.random.randint(fourth, (LAYERS,), 0, window, dtype=jnp.int32)
    offset = jnp.where(layer_ids == widest, WMAX - 1, offset)
    offset = jnp.where(layer_ids == other, 0, offset)
    return (window, offset)


def draw_windows(key, part):
    window, offset = window_plan(key)
    return window


def draw_shifts(key, part):
    window, offset = window_plan(key)
    return offset


def draw_lengths(key, part):
    key = jax.random.fold_in(key, 5)
    first, second = jax.random.split(key, 2)
    counts = jax.random.randint(first, (MICRO, UTT), CAP // 3, CAP + 1, dtype=jnp.int32)
    fullest = jax.random.randint(second, (), 0, MICRO, dtype=jnp.int32)
    rows = jnp.arange(MICRO, dtype=jnp.int32)[:, None]
    return jnp.where(rows == fullest, CAP, counts).astype(jnp.int32)


def draw_w_qkv(key, part):
    key = jax.random.fold_in(key, 11)
    first, second = jax.random.split(key, 2)
    head_width = HEADS * HDIM
    base = jnp.clip(jax.random.normal(first, (LAYERS, D, 3 * head_width), jnp.float32), -5.0, 5.0)
    spread = jnp.repeat(jax.random.uniform(second, (LAYERS, 1, 3 * HEADS), jnp.float32, 0.6, 1.6), HDIM, axis=2)
    weights = base * spread
    return (weights / jnp.sqrt(jnp.float32(D))).astype(jnp.bfloat16)


def level_of(key, shape, cuts, smallest, largest):
    level = 1.0
    for position, parts in cuts:
        steps = jax.random.uniform(jax.random.fold_in(jax.random.fold_in(key, 6), position), (parts,), jnp.float32, smallest / len(cuts), largest / len(cuts))
        level = level * jnp.repeat(jnp.exp(steps), shape[position] // parts).reshape((-1,) + (1,) * (len(shape) - 1 - position))
    return level


def scatter_about(own_key, dims, scale, reach, cuts=(), kind=jnp.bfloat16):
    array = scale * jax.random.normal(own_key, dims, jnp.float32)
    if cuts:
        array = array * level_of(own_key, dims, cuts, -0.22, 0.18)
    return jnp.clip(array, -reach, reach).astype(kind)


def setup_inputs(seed: int = 0) -> dict:
    keys = jax.random.split(jax.random.key(seed), 8)
    frames = scatter_about(keys[0], (MICRO, FRAMES, D), 1.0, 6.0, ((1, 32),))
    norm_gain = jnp.clip(1.0 + 0.1 * jax.random.normal(keys[1], (LAYERS, D), jnp.float32), 0.5, 1.5).astype(jnp.bfloat16)
    w_qkv = draw_w_qkv(jax.random.fold_in(keys[7], 71), 0)
    w_out = scatter_about(keys[3], (LAYERS, HEADS * HDIM, D), (HEADS * HDIM) ** -0.5, 0.1875, ((0, 8), (1, 32)))
    lengths = draw_lengths(jax.random.fold_in(keys[7], 71), 0)
    windows = draw_windows(jax.random.fold_in(keys[7], 71), 0)
    shifts = draw_shifts(jax.random.fold_in(keys[7], 71), 0)
    return {"frames": frames, "norm_gain": norm_gain, "w_qkv": w_qkv, "w_out": w_out, "lengths": lengths, "windows": windows, "shifts": shifts}


def apply_layer(micro_frames, slot_lengths, norm_scale, weight_qkv, weight_out, window, offset):
    frame_total = micro_frames.shape[0]
    slot_count = slot_lengths.shape[0]
    head_width = HEADS * HDIM
    input_wide = micro_frames.astype(jnp.float32)
    centre = lax.optimization_barrier(jnp.mean(input_wide, axis=-1, keepdims=True))
    centered = input_wide - centre
    variance = lax.optimization_barrier(jnp.mean(centered * centered, axis=-1, keepdims=True))
    normed = (centered * lax.rsqrt(variance + 1e-05) * norm_scale.astype(jnp.float32)).astype(jnp.bfloat16)
    projected = jnp.dot(normed, weight_qkv, preferred_element_type=jnp.float32).astype(jnp.bfloat16)
    queries = projected[:, :head_width]
    keyval = projected[:, head_width:]
    border = jnp.zeros((WMAX, 2 * head_width), jnp.bfloat16)
    padded = jnp.concatenate([border, keyval, border], axis=0)

    def valid_at(indices):
        slot_index = jnp.floor_divide(indices, CAP)
        clipped = jnp.clip(slot_index, 0, slot_count - 1)
        length_of = slot_lengths[clipped]
        inside = (indices >= 0) & (indices < frame_total)
        return (inside & (indices - slot_index * CAP < length_of), slot_index)
    all_frames = jnp.arange(frame_total, dtype=jnp.int32)
    query_valid, query_slot_all = valid_at(all_frames)
    scale = 1.0 / math.sqrt(HDIM)

    def attend_block(block_index):
        start = (block_index * FR_DEV).astype(jnp.int32)
        query_pos = start + jnp.arange(FR_DEV, dtype=jnp.int32)
        key_pos = start - WMAX + jnp.arange(FR_DEV + 2 * WMAX, dtype=jnp.int32)
        query_ok, query_slot = valid_at(query_pos)
        key_ok, key_slot = valid_at(key_pos)
        query_heads = lax.dynamic_slice_in_dim(queries, start, FR_DEV, 0).reshape(FR_DEV, HEADS, HDIM).astype(jnp.float32)
        block_kv = lax.dynamic_slice_in_dim(padded, start, FR_DEV + 2 * WMAX, 0)
        key_heads = block_kv[:, :head_width].reshape(-1, HEADS, HDIM).astype(jnp.float32)
        value_heads = block_kv[:, head_width:].reshape(-1, HEADS, HDIM).astype(jnp.float32)
        scores = jnp.einsum('qhd,khd->hqk', query_heads, key_heads) * scale
        same_window = jnp.floor_divide(query_pos - offset, window)[:, None] == jnp.floor_divide(key_pos - offset, window)[None, :]
        allowed = (query_slot[:, None] == key_slot[None, :]) & same_window & (key_ok[None, :] | (query_pos[:, None] == key_pos[None, :]))
        scores = jnp.where(allowed[None], scores, -1e+30)
        row_max = lax.optimization_barrier(jnp.max(scores, axis=-1, keepdims=True))
        weights = jnp.where(allowed[None], jnp.exp(scores - row_max), 0.0)
        probability = (weights / lax.optimization_barrier(jnp.sum(weights, axis=-1, keepdims=True))).astype(jnp.bfloat16)
        mixed = jnp.einsum('hqk,khd->qhd', probability.astype(jnp.float32), value_heads)
        return mixed.reshape(FR_DEV, head_width).astype(jnp.bfloat16)
    blocks = frame_total // FR_DEV
    mixed_all = lax.map(attend_block, jnp.arange(blocks, dtype=jnp.int32)).reshape(frame_total, head_width)
    projection = jnp.dot(mixed_all, weight_out, preferred_element_type=jnp.float32)
    return (input_wide + query_valid[:, None].astype(jnp.float32) * projection).astype(jnp.bfloat16)

def reference(frames, norm_gain, w_qkv, w_out, lengths, windows, shifts):
    current = [frames[micro_index] for micro_index in range(MICRO)]
    layer_outputs = []
    for layer_index in range(LAYERS):
        for micro_index in range(MICRO):
            current[micro_index] = apply_layer(current[micro_index], lengths[micro_index], norm_gain[layer_index], w_qkv[layer_index], w_out[layer_index], windows[layer_index], shifts[layer_index])
        layer_outputs.append(jnp.stack(current))
    return jnp.stack(layer_outputs)
```

```python
import functools
import math

import jax
import jax.numpy as jnp
from jax import lax
from jax.experimental import pallas as pl
from jax.experimental.pallas import tpu as pltpu
from jax.sharding import PartitionSpec as P

HDIM = 128
WMAX = 64
MESH = pl.DeviceIdType.MESH
NY, NZ = 4, 8
STEP = ((0, 1), (0, -1), (1, 0), (-1, 0))
FLIP = (1, 0, 3, 2)
LAG = 4
BF = jnp.bfloat16
F32 = jnp.float32


def spread_trees():
    first, second = {}, {}
    for dz in range(1, NZ):
        first[0, dz] = second[0, dz] = 0 if dz <= 4 else 1
    for dz in range(NZ):
        first[1, dz], first[2, dz], first[3, dz] = 2, 2, 3
    second[1, 0], second[2, 0], second[3, 0] = 2, 2, 3
    for dy in range(1, NY):
        for dz in range(1, NZ):
            second[dy, dz] = 0 if dz <= 4 else 1
    second[1, 4], second[2, 4], second[3, 4], second[2, 5] = 2, 2, 3, 2

    def mirrored(tree):
        return {((-y) % NY, (-z) % NZ): FLIP[d] for (y, z), d in tree.items()}

    return [first, mirrored(first), second, mirrored(second)]


def before(offset, d):
    return ((offset[0] - STEP[d][0]) % NY, (offset[1] - STEP[d][1]) % NZ)


def spread_rounds():
    trees = spread_trees()
    kids = {}
    for part, tree in enumerate(trees):
        for offset, d in tree.items():
            kids.setdefault((part, before(offset, d)), []).append((part, offset))

    def height(node):
        return 1 + max([height(k) for k in kids.get(node, [])], default=0)

    def size(node):
        return 1 + sum(size(k) for k in kids.get(node, []))

    sent = {(part, (0, 0)): -LAG for part in range(4)}
    todo = {(part, offset): d for part, tree in enumerate(trees) for offset, d in tree.items()}
    rounds = []
    while todo:
        row = [None] * 4
        for d in range(4):
            ready = [
                n for n, way in todo.items()
                if way == d and sent.get((n[0], before(n[1], d)), 10**6) + LAG <= len(rounds)
            ]
            if ready:
                row[d] = max(ready, key=lambda n: (height(n), size(n)))
        for d in range(4):
            if row[d] is not None:
                sent[row[d]] = len(rounds)
                del todo[row[d]]
        rounds.append(row)
    return rounds


def kernel(
    frames, gain, w_qkv, w_out, lengths, windows, shifts, out,
    wall, xin, kbuf, vbuf, normed, qbuf, mixed, hid,
    own_sem, spread_send, spread_recv, frame_sem, halo_send, halo_recv, hop_send, hop_recv, out_sem,
):
    section = lax.axis_index("section")
    sections = lax.axis_size("section")
    tm = lax.axis_index("tm")
    tms = lax.axis_size("tm")
    y, z = tm // NZ, tm % NZ
    micros, rows, width = xin.shape
    heads_width = kbuf.shape[2]
    heads = heads_width // HDIM
    depth = w_qkv.shape[1]
    quarter = depth // 4
    scale = math.log2(math.e) / math.sqrt(HDIM)

    def at(dy, dz):
        return ((y + dy + NY) % NY) * NZ + (z + dz + NZ) % NZ

    own = [
        pltpu.make_async_copy(w_qkv.at[0, :, pl.ds(s * heads_width, heads_width)], wall.at[p, tm], own_sem.at[p])
        for p, s in ((0, 1), (1, 2), (2, 0))
    ]
    half = depth // 2
    for i in range(2):
        own.append(
            pltpu.make_async_copy(
                w_out.at[0, :, pl.ds(i * heads_width, heads_width)],
                wall.at[3, tm, pl.ds(i * half, half)], own_sem.at[3 + i],
            )
        )
    for c in own:
        c.start()
    frame_copy = pltpu.make_async_copy(frames, xin, frame_sem)

    @pl.when(section == 0)
    def _():
        frame_copy.start()

    barrier = pltpu.get_barrier_semaphore()
    for dy, dz in STEP:
        pl.semaphore_signal(barrier, inc=1, device_id=(section, at(dy, dz)), device_id_type=MESH)
    for d in (1, -1):
        pl.semaphore_signal(barrier, inc=1, device_id=(section, (tm + d + tms) % tms), device_id_type=MESH)
        pl.semaphore_signal(
            barrier, inc=1, device_id=((section + d + sections) % sections, tm), device_id_type=MESH
        )
    pl.semaphore_wait(barrier, 8)
    for c in own:
        c.wait()

    @pl.when(tm == 0)
    def _():
        for m in range(micros):
            kbuf[m, :WMAX, :] = jnp.zeros((WMAX, heads_width), BF)
            vbuf[m, :WMAX, :] = jnp.zeros((WMAX, heads_width), BF)

    @pl.when(tm == tms - 1)
    def _():
        for m in range(micros):
            kbuf[m, WMAX + rows:, :] = jnp.zeros((WMAX, heads_width), BF)
            vbuf[m, WMAX + rows:, :] = jnp.zeros((WMAX, heads_width), BF)

    rounds = spread_rounds()

    def slot(phase, part, offset):
        source = at(-offset[0], -offset[1])
        return wall.at[pl.ds(2 * phase, 2), source, pl.ds(part * quarter, quarter)]

    def spread_copy(phase, part, offset, d):
        block = slot(phase, part, offset)
        return pltpu.make_async_remote_copy(
            src_ref=block, dst_ref=block, send_sem=spread_send.at[phase],
            recv_sem=spread_recv.at[phase, part, ((offset[0] + STEP[d][0]) % NY) * NZ + (offset[1] + STEP[d][1]) % NZ],
            device_id=(section, at(*STEP[d])), device_id_type=MESH,
        )

    def spread_arrived(phase, part, offset):
        block = slot(phase, part, offset)
        pltpu.make_async_copy(block, block, spread_recv.at[phase, part, offset[0] * NZ + offset[1]]).wait()

    def spread(phase, _):
        seen = {(part, (0, 0)) for part in range(4)}
        for row in rounds:
            for d, node in enumerate(row):
                if node is None:
                    continue
                part, offset = node
                source = (part, before(offset, d))
                if source not in seen:
                    spread_arrived(phase, *source)
                    seen.add(source)
                spread_copy(phase, part, source[1], d).start()
        for part in range(4):
            for o in range(1, NY * NZ):
                node = (part, (o // NZ, o % NZ))
                if node not in seen:
                    spread_arrived(phase, *node)
        return 0

    lax.fori_loop(0, 2, spread, 0)
    for phase in range(2):
        sent = wall.at[pl.ds(2 * phase, 2), pl.ds(0, NY * NZ - 1)]
        pltpu.make_async_copy(sent, sent, spread_send.at[phase]).wait()

    window = windows[section]
    shift = shifts[section]

    def window_of(pos):
        n = pos - shift
        guess = jnp.floor((n.astype(F32) + 0.5) / window.astype(F32)).astype(jnp.int32)
        rest = n - guess * window
        return guess + (rest >= window).astype(jnp.int32) - (rest < 0).astype(jnp.int32)

    query_pos = tm * rows + lax.broadcasted_iota(jnp.int32, (rows, 1), 0)
    key_pos = tm * rows - WMAX + lax.broadcasted_iota(jnp.int32, (1, rows + 2 * WMAX), 1)
    total = rows * tms
    near = (window_of(query_pos) == window_of(key_pos)) & (key_pos >= 0) & (key_pos < total)
    same = query_pos == key_pos

    def halo(m, kind, side):
        buf = (kbuf, vbuf)[kind]
        src = (rows, WMAX)[side]
        dst = (0, WMAX + rows)[side]
        return pltpu.make_async_remote_copy(
            src_ref=buf.at[m, pl.ds(src, WMAX)], dst_ref=buf.at[m, pl.ds(dst, WMAX)],
            send_sem=halo_send.at[m, kind, side], recv_sem=halo_recv.at[m, kind, side],
            device_id=(section, (tm + (1, -1)[side] + tms) % tms), device_id_type=MESH,
        )

    def halo_start(m, kind):
        @pl.when(tm < tms - 1)
        def _():
            halo(m, kind, 0).start()

        @pl.when(tm > 0)
        def _():
            halo(m, kind, 1).start()

    def halo_arrived(m, kind):
        @pl.when(tm > 0)
        def _():
            halo(m, kind, 0).wait_recv()

        @pl.when(tm < tms - 1)
        def _():
            halo(m, kind, 1).wait_recv()

    chunk = heads_width // 2
    chunks = width // chunk

    def hop(m, c):
        return pltpu.make_async_remote_copy(
            src_ref=hid.at[m, :, pl.ds(c * chunk, chunk)], dst_ref=xin.at[m, :, pl.ds(c * chunk, chunk)],
            send_sem=hop_send.at[m, c], recv_sem=hop_recv.at[m, c],
            device_id=((section + 1) % sections, tm), device_id_type=MESH,
        )

    @pl.when(section == 0)
    def _():
        frame_copy.wait()

    def project(slab, col):
        w = wall[slab, :, :, col:col + chunk].reshape(width, chunk)
        return jnp.dot(normed[...], w, preferred_element_type=F32).astype(BF)

    def stage(m, _):
        @pl.when(section > 0)
        def _():
            for c in range(chunks):
                hop(m, c).wait_recv()

        x = xin[m].astype(F32)
        centered = x - jnp.mean(x, axis=-1, keepdims=True)
        variance = jnp.mean(centered * centered, axis=-1, keepdims=True)
        normed[...] = (centered * lax.rsqrt(variance + 1e-05) * gain[...].astype(F32)).astype(BF)
        for kind, buf in enumerate((kbuf, vbuf)):
            for col in range(0, heads_width, chunk):
                buf[m, WMAX:WMAX + rows, col:col + chunk] = project(kind, col)
            halo_start(m, kind)
        for col in range(0, heads_width, chunk):
            qbuf[:, col:col + chunk] = project(2, col)
        length = lengths[m, 0]
        allowed = near & ((key_pos < length) | same)
        halo_arrived(m, 0)
        halo_arrived(m, 1)
        for h in range(heads):
            cols = slice(h * HDIM, (h + 1) * HDIM)
            scores = lax.dot_general(
                qbuf[:, cols], kbuf[m, :, cols], (((1,), (1,)), ((), ())), preferred_element_type=F32
            )
            scores = jnp.where(allowed, scores, -1e30)
            weights = jnp.exp2((scores - jnp.max(scores, axis=-1, keepdims=True)) * scale)
            total_weight = jnp.sum(weights, axis=-1, keepdims=True)
            head = jnp.dot(weights.astype(BF), vbuf[m, :, cols], preferred_element_type=F32)
            mixed[:, cols] = (head / total_weight).astype(BF)
        valid = (query_pos < length).astype(F32)
        for c in range(chunks):
            part, col = c * chunk // heads_width, c * chunk % heads_width
            w = wall[3, :, part * half:(part + 1) * half, col:col + chunk].reshape(heads_width, chunk)
            projection = jnp.dot(mixed[...], w, preferred_element_type=F32)
            cols = slice(c * chunk, (c + 1) * chunk)
            hid[m, :, cols] = (xin[m, :, cols].astype(F32) + valid * projection).astype(BF)

            @pl.when(section < sections - 1)
            def _():
                hop(m, c).start()

        pltpu.make_async_copy(hid.at[m], out.at[0, m], out_sem.at[m]).start()
        return 0

    lax.fori_loop(0, micros, stage, 0)

    def finish(m, _):
        pltpu.make_async_copy(hid.at[m], out.at[0, m], out_sem.at[m]).wait()
        for kind in range(2):
            @pl.when(tm < tms - 1)
            def _():
                halo(m, kind, 0).wait_send()

            @pl.when(tm > 0)
            def _():
                halo(m, kind, 1).wait_send()

        @pl.when(section < sections - 1)
        def _():
            for c in range(chunks):
                hop(m, c).wait_send()

        return 0

    lax.fori_loop(0, micros, finish, 0)


def on_device(frames, norm_gain, w_qkv, w_out, lengths, windows, shifts):
    micros, rows, width = frames.shape
    depth = w_qkv.shape[1]
    heads_width = w_qkv.shape[2] // 3
    tms = lax.axis_size("tm")
    dma = pltpu.SemaphoreType.DMA
    vmem = pl.BlockSpec(memory_space=pltpu.VMEM)
    smem = pl.BlockSpec(memory_space=pltpu.SMEM)
    hbm = pl.BlockSpec(memory_space=pl.ANY)
    keys = rows + 2 * WMAX
    return pl.pallas_call(
        kernel,
        out_shape=jax.ShapeDtypeStruct((1, micros, rows, width), BF),
        in_specs=[hbm, vmem, hbm, hbm, smem, smem, smem],
        out_specs=hbm,
        scratch_shapes=[
            pltpu.VMEM((4, tms, depth, heads_width), BF),
            pltpu.VMEM((micros, rows, width), BF),
            pltpu.VMEM((micros, keys, heads_width), BF),
            pltpu.VMEM((micros, keys, heads_width), BF),
            pltpu.VMEM((rows, width), BF),
            pltpu.VMEM((rows, heads_width), BF),
            pltpu.VMEM((rows, heads_width), BF),
            pltpu.VMEM((micros, rows, width), BF),
            dma((5,)), dma((2,)), dma((2, 4, tms)), dma,
            dma((micros, 2, 2)), dma((micros, 2, 2)), dma((micros, 4)), dma((micros, 4)), dma((micros,)),
        ],
        compiler_params=pltpu.CompilerParams(
            collective_id=0, has_side_effects=True, vmem_limit_bytes=52 << 20
        ),
        name="relay",
    )(frames, norm_gain, w_qkv, w_out, lengths, windows, shifts)


def solution(mesh):
    return jax.shard_map(
        on_device,
        mesh=mesh,
        in_specs=(
            P(None, "tm", None),
            P("section", None),
            P("section", "tm", None),
            P("section", "tm", None),
            P(),
            P(),
            P(),
        ),
        out_specs=P("section", None, "tm", None),
        check_vma=False,
    )
```

```python
import functools
import math

import jax
import jax.numpy as jnp
from jax import lax
from jax.experimental import pallas as pl
from jax.experimental.pallas import tpu as pltpu
from jax.sharding import PartitionSpec as P

HDIM = 128
WMAX = 64
MESH = pl.DeviceIdType.MESH
NY, NZ = 4, 8
STEP = ((0, 1), (0, -1), (1, 0), (-1, 0))
FLIP = (1, 0, 3, 2)
LAG = 5
GROUP = 2 * HDIM
LENT = 3 * HDIM
BF = jnp.bfloat16
F32 = jnp.float32


def spread_trees():
    first, second = {}, {}
    for dz in range(1, NZ):
        first[0, dz] = second[0, dz] = 0 if dz <= 4 else 1
    for dz in range(NZ):
        first[1, dz], first[2, dz], first[3, dz] = 2, 2, 3
    second[1, 0], second[2, 0], second[3, 0] = 2, 2, 3
    for dy in range(1, NY):
        for dz in range(1, NZ):
            second[dy, dz] = 0 if dz <= 4 else 1
    second[1, 4], second[2, 4], second[3, 4], second[2, 5] = 2, 2, 3, 2

    def mirrored(tree):
        return {((-y) % NY, (-z) % NZ): FLIP[d] for (y, z), d in tree.items()}

    return [first, mirrored(first), second, mirrored(second)]


def before(offset, d):
    return ((offset[0] - STEP[d][0]) % NY, (offset[1] - STEP[d][1]) % NZ)


def spread_rounds():
    trees = spread_trees()
    kids = {}
    for part, tree in enumerate(trees):
        for offset, d in tree.items():
            kids.setdefault((part, before(offset, d)), []).append((part, offset))

    def height(node):
        return 1 + max([height(k) for k in kids.get(node, [])], default=0)

    def size(node):
        return 1 + sum(size(k) for k in kids.get(node, []))

    sent = {(part, (0, 0)): -LAG for part in range(4)}
    todo = {(part, offset): d for part, tree in enumerate(trees) for offset, d in tree.items()}
    rounds = []
    while todo:
        row = [None] * 4
        for d in range(4):
            ready = [
                n for n, way in todo.items()
                if way == d and sent.get((n[0], before(n[1], d)), 10**6) + LAG <= len(rounds)
            ]
            if ready:
                row[d] = max(ready, key=lambda n: (height(n), size(n)))
        for d in range(4):
            if row[d] is not None:
                sent[row[d]] = len(rounds)
                del todo[row[d]]
        rounds.append(row)
    return rounds


def kernel(
    frames, gain_hbm, w_qkv, w_out, lengths_hbm, windows_hbm, shifts_hbm, out,
    wall, lent, xin, kv, normed, qbuf, mixed, hid, gain, lengths, windows, shifts,
    own_sem, small_sem, spread_send, spread_recv, lend_sem, lent_send, lent_recv, frame_sem, halo_send, halo_recv, hop_send, hop_recv,
    out_sem,
):
    section = lax.axis_index("section")
    sections = lax.axis_size("section")
    tm = lax.axis_index("tm")
    tms = lax.axis_size("tm")
    y, z = tm // NZ, tm % NZ
    micros, rows, width = xin.shape
    heads_width = wall.shape[3]
    groups = heads_width // GROUP
    depth = w_qkv.shape[1]
    quarter, half = depth // 4, depth // 2
    pair = 2 * GROUP
    pairs = heads_width // pair
    scale = math.log2(math.e) / math.sqrt(HDIM)

    def at(dy, dz):
        return ((y + dy + NY) % NY) * NZ + (z + dz + NZ) % NZ

    own = []

    def take(source, target):
        own.append(pltpu.make_async_copy(source, target, own_sem.at[len(own)]))

    for g in range(groups):
        for kind in range(2):
            take(
                w_qkv.at[0, :, pl.ds((1 + kind) * heads_width + g * GROUP, GROUP)],
                wall.at[g // pairs, tm, :, pl.ds(g % pairs * pair + kind * GROUP, GROUP)],
            )
    take(w_qkv.at[0, :, pl.ds(0, heads_width)], wall.at[2, tm])
    for i in range(2):
        take(w_out.at[0, :, pl.ds(i * heads_width, heads_width)], wall.at[3, tm, pl.ds(i * half, half)])
    small = [
        pltpu.make_async_copy(source, target, small_sem.at[i])
        for i, (source, target) in enumerate(
            ((gain_hbm, gain), (lengths_hbm, lengths), (windows_hbm, windows), (shifts_hbm, shifts))
        )
    ]
    for c in own + small:
        c.start()
    frame_copy = pltpu.make_async_copy(frames, xin, frame_sem)

    @pl.when(section == 0)
    def _():
        frame_copy.start()

    barrier = pltpu.get_barrier_semaphore()
    for dy, dz in STEP:
        pl.semaphore_signal(barrier, inc=1, device_id=(section, at(dy, dz)), device_id_type=MESH)
    for d in (1, -1):
        pl.semaphore_signal(barrier, inc=1, device_id=(section, (tm + d + tms) % tms), device_id_type=MESH)
    for d in (1, -1, 2, -2):
        pl.semaphore_signal(
            barrier, inc=1, device_id=((section + d + sections) % sections, tm), device_id_type=MESH
        )

    @pl.when(tm == 0)
    def _():
        for m in range(micros):
            kv[m, :WMAX, :] = jnp.zeros((WMAX, 2 * heads_width), BF)

    @pl.when(tm == tms - 1)
    def _():
        for m in range(micros):
            kv[m, WMAX + rows:, :] = jnp.zeros((WMAX, 2 * heads_width), BF)

    borrows, lends = section < 2, section >= sections - 2

    for c in small + own:
        c.wait()
    pl.semaphore_wait(barrier, 10)

    @pl.when(section == 0)
    def _():
        frame_copy.wait()

    window = windows[section]
    shift = shifts[section]

    def window_of(pos):
        n = pos - shift
        guess = jnp.floor((n.astype(F32) + 0.5) / window.astype(F32)).astype(jnp.int32)
        rest = n - guess * window
        return guess + (rest >= window).astype(jnp.int32) - (rest < 0).astype(jnp.int32)

    query_pos = tm * rows + lax.broadcasted_iota(jnp.int32, (rows, 1), 0)
    key_pos = tm * rows - WMAX + lax.broadcasted_iota(jnp.int32, (1, rows + 2 * WMAX), 1)
    same = query_pos == key_pos

    def halo(m, g, side):
        src = (rows, WMAX)[side]
        dst = (0, WMAX + rows)[side]
        return pltpu.make_async_remote_copy(
            src_ref=kv.at[m, pl.ds(src, WMAX), pl.ds(g * pair, pair)],
            dst_ref=kv.at[m, pl.ds(dst, WMAX), pl.ds(g * pair, pair)],
            send_sem=halo_send.at[m, g, side], recv_sem=halo_recv.at[m, g, side],
            device_id=(section, (tm + (1, -1)[side] + tms) % tms), device_id_type=MESH,
        )

    def each_side(act, before_me, after_me):
        @pl.when(tm < tms - 1)
        def _():
            act(after_me)

        @pl.when(tm > 0)
        def _():
            act(before_me)

    chunk = heads_width // 2
    chunks = width // chunk

    def hop(m, c):
        return pltpu.make_async_remote_copy(
            src_ref=hid.at[m, :, pl.ds(c * chunk, chunk)], dst_ref=xin.at[m, :, pl.ds(c * chunk, chunk)],
            send_sem=hop_send.at[m, c], recv_sem=hop_recv.at[m, c],
            device_id=((section + 1) % sections, tm), device_id_type=MESH,
        )

    def project(slab, col):
        w = wall[slab, :, :, col:col + pair].reshape(width, pair)
        return jnp.dot(normed[...], w, preferred_element_type=F32).astype(BF)

    def enter(m):
        @pl.when(section > 0)
        def _():
            for c in range(chunks):
                hop(m, c).wait_recv()

        x = xin[m].astype(F32)
        centered = x - jnp.mean(x, axis=-1, keepdims=True)
        variance = jnp.mean(centered * centered, axis=-1, keepdims=True)
        normed[...] = (centered * lax.rsqrt(variance + 1e-05) * gain[...].astype(F32)).astype(BF)

    def keys_values(m, slab, i):
        g = slab * pairs + i
        cols = pl.ds(pl.multiple_of(g * pair, pair), pair)
        kv[m, pl.ds(WMAX, rows), cols] = project(slab, i * pair)
        each_side(lambda side: halo(m, g, side).start(), 1, 0)

    rounds = spread_rounds()
    near_cols = heads_width - LENT
    lent_cols = pl.ds(near_cols, LENT)

    def blocks(phase, source, first, count):
        line = pl.ds(first, count)
        if phase == 0:
            return wall.at[pl.ds(0, 2), source, line]
        if phase == 1:
            return wall.at[pl.ds(2, 2), source, line, pl.ds(0, near_cols)]
        if phase == 2:
            return wall.at[pl.ds(2, 2), source, line, lent_cols]
        return lent.at[:, source, line]

    def slot(phase, part, offset):
        return blocks(phase, at(-offset[0], -offset[1]), part * quarter, quarter)

    def spread_copy(phase, part, offset, d):
        block = slot(phase, part, offset)
        return pltpu.make_async_remote_copy(
            src_ref=block, dst_ref=block, send_sem=spread_send.at[phase],
            recv_sem=spread_recv.at[phase, part, ((offset[0] + STEP[d][0]) % NY) * NZ + (offset[1] + STEP[d][1]) % NZ],
            device_id=(section, at(*STEP[d])), device_id_type=MESH,
        )

    def lend():
        return pltpu.make_async_remote_copy(
            src_ref=blocks(2, tm, 0, depth), dst_ref=blocks(3, tm, 0, depth), send_sem=lend_sem.at[0],
            recv_sem=lend_sem.at[1], device_id=((section + sections - 2) % sections, tm), device_id_type=MESH,
        )

    def spread_arrived(phase, part, offset):
        block = slot(phase, part, offset)
        pltpu.make_async_copy(block, block, spread_recv.at[phase, part, offset[0] * NZ + offset[1]]).wait()
        if phase == 3:
            pltpu.make_async_remote_copy(
                src_ref=block, dst_ref=slot(2, part, offset), send_sem=lent_send, recv_sem=lent_recv,
                device_id=((section + 2) % sections, tm), device_id_type=MESH,
            ).start()

    def spread(phase, behind=()):
        seen = {(part, (0, 0)) for part in range(4)}
        for r, row in enumerate(rounds):
            if r == LAG:
                for node in behind:
                    spread_arrived(*node)
            for d, node in enumerate(row):
                if node is None:
                    continue
                part, source = node[0], before(node[1], d)
                if (part, source) not in seen:
                    spread_arrived(phase, part, source)
                    seen.add((part, source))
                spread_copy(phase, part, source, d).start()
        every = [(part, (o // NZ, o % NZ)) for part in range(4) for o in range(1, NY * NZ)]
        return [(phase, *node) for node in every if node not in seen]

    def spread_sent(phase):
        if phase == 3:
            sent = lent.at[:, pl.ds(0, NY * NZ - 1)]
        elif phase == 0:
            sent = wall.at[pl.ds(0, 2), pl.ds(0, NY * NZ - 1)]
        else:
            sent = wall.at[pl.ds(2, 2), pl.ds(0, NY * NZ - 1), :, pl.ds(0, near_cols) if phase == 1 else lent_cols]
        return sent

    def all_sent(phase):
        sent = spread_sent(phase)
        pltpu.make_async_copy(sent, sent, spread_send.at[phase]).wait()

    @pl.when(borrows)
    def _():
        lend().start()

    @pl.when(lends)
    def _():
        lend().wait_recv()
        for node in spread(3):
            spread_arrived(*node)

    for node in spread(1, spread(0)):
        spread_arrived(*node)

    @pl.when(borrows)
    def _():
        lend().wait_send()
        sent = spread_sent(2)
        pltpu.make_async_copy(sent, sent, lent_recv).wait()

    @pl.when(section >= 2)
    def _():
        for node in spread(2):
            spread_arrived(*node)

    def queries(m):
        for col in range(0, heads_width, pair):
            qbuf[m, :, col:col + pair] = project(2, col)

    def attend(m):
        length = lengths[m, 0]
        near = (window_of(query_pos) == window_of(key_pos)) & (key_pos >= 0) & (key_pos < rows * tms)
        allowed = near & ((key_pos < length) | same)
        valid = (query_pos < length).astype(F32)
        for h in range(heads_width // HDIM):
            qcol = h * HDIM
            if qcol % (heads_width // 2) == 0:
                for g in range(qcol // GROUP, (qcol + heads_width // 2) // GROUP):
                    each_side(lambda side: halo(m, g, side).wait_recv(), 0, 1)
            kcol = qcol // GROUP * pair + qcol % GROUP
            vcol = kcol + GROUP
            scores = lax.dot_general(
                qbuf[m, :, qcol:qcol + HDIM], kv[m, :, kcol:kcol + HDIM], (((1,), (1,)), ((), ())),
                preferred_element_type=F32,
            )
            scores = jnp.where(allowed, scores, -1e30)
            weights = jnp.exp2((scores - jnp.max(scores, axis=-1, keepdims=True)) * scale)
            total_weight = jnp.sum(weights, axis=-1, keepdims=True)
            head = jnp.dot(weights.astype(BF), kv[m, :, vcol:vcol + HDIM], preferred_element_type=F32)
            mixed[:, qcol:qcol + HDIM] = (head / total_weight).astype(BF)
        for c in range(chunks):
            part, col = c * chunk // heads_width, c * chunk % heads_width
            w = wall[3, :, part * half:(part + 1) * half, col:col + chunk].reshape(heads_width, chunk)
            cols = slice(c * chunk, (c + 1) * chunk)
            projection = jnp.dot(mixed[...], w, preferred_element_type=F32)
            hid[m, :, cols] = (xin[m, :, cols].astype(F32) + valid * projection).astype(BF)

            @pl.when(section < sections - 1)
            def _():
                hop(m, c).start()

        pltpu.make_async_copy(hid.at[m], out.at[0, m], out_sem.at[m]).start()

    def stage(i, _):
        @pl.when(i < micros)
        def _():
            enter(i)
            for slab in range(2):
                for j in range(pairs):
                    keys_values(i, slab, j)
            queries(i)

        @pl.when(i > 0)
        def _():
            attend(i - 1)

        return 0

    lax.fori_loop(0, micros + 1, stage, 0)

    for phase in range(2):
        all_sent(phase)

    @pl.when(section >= 2)
    def _():
        all_sent(2)

    @pl.when(lends)
    def _():
        all_sent(3)
        sent = spread_sent(3)
        pltpu.make_async_copy(sent, sent, lent_send).wait()

    def finish(m, _):
        pltpu.make_async_copy(hid.at[m], out.at[0, m], out_sem.at[m]).wait()
        for g in range(groups):
            each_side(lambda side: halo(m, g, side).wait_send(), 1, 0)

        @pl.when(section < sections - 1)
        def _():
            for c in range(chunks):
                hop(m, c).wait_send()

        return 0

    lax.fori_loop(0, micros, finish, 0)


def on_device(frames, norm_gain, w_qkv, w_out, lengths, windows, shifts):
    micros, rows, width = frames.shape
    depth = w_qkv.shape[1]
    heads_width = w_qkv.shape[2] // 3
    groups = heads_width // GROUP
    tms = lax.axis_size("tm")
    dma = pltpu.SemaphoreType.DMA
    hbm = pl.BlockSpec(memory_space=pl.ANY)
    return pl.pallas_call(
        kernel,
        out_shape=jax.ShapeDtypeStruct((1, micros, rows, width), BF),
        in_specs=[hbm] * 7,
        out_specs=hbm,
        scratch_shapes=[
            pltpu.VMEM((4, tms, depth, heads_width), BF),
            pltpu.VMEM((2, tms, depth, LENT), BF),
            pltpu.VMEM((micros, rows, width), BF),
            pltpu.VMEM((micros, rows + 2 * WMAX, 2 * heads_width), BF),
            pltpu.VMEM((rows, width), BF),
            pltpu.VMEM((micros, rows, heads_width), BF),
            pltpu.VMEM((rows, heads_width), BF),
            pltpu.VMEM((micros, rows, width), BF),
            pltpu.VMEM(norm_gain.shape, BF),
            pltpu.SMEM(lengths.shape, jnp.int32),
            pltpu.SMEM(windows.shape, jnp.int32),
            pltpu.SMEM(shifts.shape, jnp.int32),
            dma((2 * groups + 3,)), dma((4,)), dma((4,)), dma((4, 4, tms)), dma((2,)), dma, dma, dma,
            dma((micros, groups, 2)), dma((micros, groups, 2)), dma((micros, 4)), dma((micros, 4)), dma((micros,)),
        ],
        compiler_params=pltpu.CompilerParams(
            collective_id=0, has_side_effects=True, vmem_limit_bytes=52 << 20
        ),
        name="relay",
    )(frames, norm_gain, w_qkv, w_out, lengths, windows, shifts)


def solution(mesh):
    return jax.shard_map(
        on_device,
        mesh=mesh,
        in_specs=(
            P(None, "tm", None),
            P("section", None),
            P("section", "tm", None),
            P("section", "tm", None),
            P(),
            P(),
            P(),
        ),
        out_specs=P("section", None, "tm", None),
        check_vma=False,
    )
```

```python
import functools
import math

import jax
import jax.numpy as jnp
from jax import lax
from jax.experimental import pallas as pl
from jax.experimental.pallas import tpu as pltpu
from jax.sharding import PartitionSpec as P

HDIM = 128
WMAX = 64
MESH = pl.DeviceIdType.MESH
NY, NZ = 4, 8
STEP = ((0, 1), (0, -1), (1, 0), (-1, 0))
FLIP = (1, 0, 3, 2)
LAG = 5
GROUP = 2 * HDIM
LENT = 3 * HDIM
BF = jnp.bfloat16
F32 = jnp.float32


def spread_trees():
    first, second = {}, {}
    for dz in range(1, NZ):
        first[0, dz] = second[0, dz] = 0 if dz <= 4 else 1
    for dz in range(NZ):
        first[1, dz], first[2, dz], first[3, dz] = 2, 2, 3
    second[1, 0], second[2, 0], second[3, 0] = 2, 2, 3
    for dy in range(1, NY):
        for dz in range(1, NZ):
            second[dy, dz] = 0 if dz <= 4 else 1
    second[1, 4], second[2, 4], second[3, 4], second[2, 5] = 2, 2, 3, 2

    def mirrored(tree):
        return {((-y) % NY, (-z) % NZ): FLIP[d] for (y, z), d in tree.items()}

    return [first, mirrored(first), second, mirrored(second)]


def before(offset, d):
    return ((offset[0] - STEP[d][0]) % NY, (offset[1] - STEP[d][1]) % NZ)


def spread_rounds():
    trees = spread_trees()
    kids = {}
    for part, tree in enumerate(trees):
        for offset, d in tree.items():
            kids.setdefault((part, before(offset, d)), []).append((part, offset))

    def height(node):
        return 1 + max([height(k) for k in kids.get(node, [])], default=0)

    def size(node):
        return 1 + sum(size(k) for k in kids.get(node, []))

    sent = {(part, (0, 0)): -LAG for part in range(4)}
    todo = {(part, offset): d for part, tree in enumerate(trees) for offset, d in tree.items()}
    rounds = []
    while todo:
        row = [None] * 4
        for d in range(4):
            ready = [
                n for n, way in todo.items()
                if way == d and sent.get((n[0], before(n[1], d)), 10**6) + LAG <= len(rounds)
            ]
            if ready:
                row[d] = max(ready, key=lambda n: (height(n), size(n)))
        for d in range(4):
            if row[d] is not None:
                sent[row[d]] = len(rounds)
                del todo[row[d]]
        rounds.append(row)
    return rounds


def kernel(
    frames, gain_hbm, w_qkv, w_out, lengths_hbm, windows_hbm, shifts_hbm, out,
    wall, lent, xin, kv, normed, qbuf, mixed, hid, gain, lengths, windows, shifts,
    own_sem, small_sem, spread_send, spread_recv, lend_sem, lent_send, lent_recv, frame_sem, halo_send, halo_recv, hop_send, hop_recv,
    out_sem,
):
    section = lax.axis_index("section")
    sections = lax.axis_size("section")
    tm = lax.axis_index("tm")
    tms = lax.axis_size("tm")
    y, z = tm // NZ, tm % NZ
    micros, rows, width = xin.shape
    heads_width = wall.shape[3]
    groups = heads_width // GROUP
    depth = w_qkv.shape[1]
    quarter, half = depth // 4, depth // 2
    pair = 2 * GROUP
    pairs = heads_width // pair
    scale = math.log2(math.e) / math.sqrt(HDIM)

    def at(dy, dz):
        return ((y + dy + NY) % NY) * NZ + (z + dz + NZ) % NZ

    own = []

    def take(source, target):
        own.append(pltpu.make_async_copy(source, target, own_sem.at[len(own)]))

    for g in range(groups):
        for kind in range(2):
            take(
                w_qkv.at[0, :, pl.ds((1 + kind) * heads_width + g * GROUP, GROUP)],
                wall.at[g // pairs, tm, :, pl.ds(g % pairs * pair + kind * GROUP, GROUP)],
            )
    take(w_qkv.at[0, :, pl.ds(0, heads_width)], wall.at[2, tm])
    for i in range(2):
        take(w_out.at[0, :, pl.ds(i * heads_width, heads_width)], wall.at[3, tm, pl.ds(i * half, half)])
    small = [
        pltpu.make_async_copy(source, target, small_sem.at[i])
        for i, (source, target) in enumerate(
            ((gain_hbm, gain), (lengths_hbm, lengths), (windows_hbm, windows), (shifts_hbm, shifts))
        )
    ]
    for c in own + small:
        c.start()
    frame_copy = pltpu.make_async_copy(frames, xin, frame_sem)

    @pl.when(section == 0)
    def _():
        frame_copy.start()

    barrier = pltpu.get_barrier_semaphore()
    for dy, dz in STEP:
        pl.semaphore_signal(barrier, inc=1, device_id=(section, at(dy, dz)), device_id_type=MESH)
    for d in (1, -1):
        pl.semaphore_signal(barrier, inc=1, device_id=(section, (tm + d + tms) % tms), device_id_type=MESH)
    for d in (1, -1, 2, -2):
        pl.semaphore_signal(
            barrier, inc=1, device_id=((section + d + sections) % sections, tm), device_id_type=MESH
        )

    @pl.when(tm == 0)
    def _():
        for m in range(micros):
            kv[m, :WMAX, :] = jnp.zeros((WMAX, 2 * heads_width), BF)

    @pl.when(tm == tms - 1)
    def _():
        for m in range(micros):
            kv[m, WMAX + rows:, :] = jnp.zeros((WMAX, 2 * heads_width), BF)

    borrows, lends = section < 2, section >= sections - 2

    for c in small + own:
        c.wait()
    pl.semaphore_wait(barrier, 10)

    @pl.when(section == 0)
    def _():
        frame_copy.wait()

    window = windows[section]
    shift = shifts[section]

    def window_of(pos):
        n = pos - shift
        guess = jnp.floor((n.astype(F32) + 0.5) / window.astype(F32)).astype(jnp.int32)
        rest = n - guess * window
        return guess + (rest >= window).astype(jnp.int32) - (rest < 0).astype(jnp.int32)

    query_pos = tm * rows + lax.broadcasted_iota(jnp.int32, (rows, 1), 0)
    key_pos = tm * rows - WMAX + lax.broadcasted_iota(jnp.int32, (1, rows + 2 * WMAX), 1)
    same = query_pos == key_pos

    def halo(m, g, side):
        src = (rows, WMAX)[side]
        dst = (0, WMAX + rows)[side]
        return pltpu.make_async_remote_copy(
            src_ref=kv.at[m, pl.ds(src, WMAX), pl.ds(g * pair, pair)],
            dst_ref=kv.at[m, pl.ds(dst, WMAX), pl.ds(g * pair, pair)],
            send_sem=halo_send.at[m, g, side], recv_sem=halo_recv.at[m, g, side],
            device_id=(section, (tm + (1, -1)[side] + tms) % tms), device_id_type=MESH,
        )

    def each_side(act, before_me, after_me):
        @pl.when(tm < tms - 1)
        def _():
            act(after_me)

        @pl.when(tm > 0)
        def _():
            act(before_me)

    chunk = heads_width // 2
    chunks = width // chunk

    def hop(m, c):
        return pltpu.make_async_remote_copy(
            src_ref=hid.at[m, :, pl.ds(c * chunk, chunk)], dst_ref=xin.at[m, :, pl.ds(c * chunk, chunk)],
            send_sem=hop_send.at[m, c], recv_sem=hop_recv.at[m, c],
            device_id=((section + 1) % sections, tm), device_id_type=MESH,
        )

    def project(slab, col):
        w = wall[slab, :, :, col:col + pair].reshape(width, pair)
        return jnp.dot(normed[...], w, preferred_element_type=F32).astype(BF)

    def enter(m):
        @pl.when(section > 0)
        def _():
            for c in range(chunks):
                hop(m, c).wait_recv()

        x = xin[m].astype(F32)
        centered = x - jnp.mean(x, axis=-1, keepdims=True)
        variance = jnp.mean(centered * centered, axis=-1, keepdims=True)
        normed[...] = (centered * lax.rsqrt(variance + 1e-05) * gain[...].astype(F32)).astype(BF)

    def keys_values(m, slab, i):
        g = slab * pairs + i
        cols = pl.ds(pl.multiple_of(g * pair, pair), pair)
        kv[m, pl.ds(WMAX, rows), cols] = project(slab, i * pair)
        each_side(lambda side: halo(m, g, side).start(), 1, 0)

    rounds = spread_rounds()
    near_cols = heads_width - LENT
    lent_cols = pl.ds(near_cols, LENT)

    def blocks(phase, source, first, count):
        line = pl.ds(first, count)
        if phase == 0:
            return wall.at[pl.ds(0, 2), source, line]
        if phase == 1:
            return wall.at[pl.ds(2, 2), source, line, pl.ds(0, near_cols)]
        if phase == 2:
            return wall.at[pl.ds(2, 2), source, line, lent_cols]
        return lent.at[:, source, line]

    def slot(phase, part, offset):
        return blocks(phase, at(-offset[0], -offset[1]), part * quarter, quarter)

    def spread_copy(phase, part, offset, d):
        block = slot(phase, part, offset)
        return pltpu.make_async_remote_copy(
            src_ref=block, dst_ref=block, send_sem=spread_send.at[phase],
            recv_sem=spread_recv.at[phase, part, ((offset[0] + STEP[d][0]) % NY) * NZ + (offset[1] + STEP[d][1]) % NZ],
            device_id=(section, at(*STEP[d])), device_id_type=MESH,
        )

    def lend():
        return pltpu.make_async_remote_copy(
            src_ref=blocks(2, tm, 0, depth), dst_ref=blocks(3, tm, 0, depth), send_sem=lend_sem.at[0],
            recv_sem=lend_sem.at[1], device_id=((section + sections - 2) % sections, tm), device_id_type=MESH,
        )

    def spread_arrived(phase, part, offset):
        block = slot(phase, part, offset)
        pltpu.make_async_copy(block, block, spread_recv.at[phase, part, offset[0] * NZ + offset[1]]).wait()
        if phase == 3:
            pltpu.make_async_remote_copy(
                src_ref=block, dst_ref=slot(2, part, offset), send_sem=lent_send, recv_sem=lent_recv,
                device_id=((section + 2) % sections, tm), device_id_type=MESH,
            ).start()

    def spread(phase, behind=()):
        seen = {(part, (0, 0)) for part in range(4)}
        for r, row in enumerate(rounds):
            if r == LAG:
                for node in behind:
                    spread_arrived(*node)
            for d, node in enumerate(row):
                if node is None:
                    continue
                part, source = node[0], before(node[1], d)
                if (part, source) not in seen:
                    spread_arrived(phase, part, source)
                    seen.add((part, source))
                spread_copy(phase, part, source, d).start()
        every = [(part, (o // NZ, o % NZ)) for part in range(4) for o in range(1, NY * NZ)]
        return [(phase, *node) for node in every if node not in seen]

    def spread_sent(phase):
        if phase == 3:
            sent = lent.at[:, pl.ds(0, NY * NZ - 1)]
        elif phase == 0:
            sent = wall.at[pl.ds(0, 2), pl.ds(0, NY * NZ - 1)]
        else:
            sent = wall.at[pl.ds(2, 2), pl.ds(0, NY * NZ - 1), :, pl.ds(0, near_cols) if phase == 1 else lent_cols]
        return sent

    def all_sent(phase):
        sent = spread_sent(phase)
        pltpu.make_async_copy(sent, sent, spread_send.at[phase]).wait()

    @pl.when(borrows)
    def _():
        lend().start()

    @pl.when(lends)
    def _():
        lend().wait_recv()
        for node in spread(3):
            spread_arrived(*node)

    for node in spread(1, spread(0)):
        spread_arrived(*node)

    @pl.when(borrows)
    def _():
        lend().wait_send()
        sent = spread_sent(2)
        pltpu.make_async_copy(sent, sent, lent_recv).wait()

    @pl.when(section >= 2)
    def _():
        for node in spread(2):
            spread_arrived(*node)

    def queries(m):
        for col in range(0, heads_width, pair):
            qbuf[m, :, col:col + pair] = project(2, col)

    def attend(m):
        length = lengths[m]
        near = (window_of(query_pos) == window_of(key_pos)) & (key_pos >= 0) & (key_pos < rows * tms)
        allowed = near & ((key_pos < length) | same)
        valid = (query_pos < length).astype(F32)
        for h in range(heads_width // HDIM):
            qcol = h * HDIM
            if qcol % (heads_width // 2) == 0:
                for g in range(qcol // GROUP, (qcol + heads_width // 2) // GROUP):
                    each_side(lambda side: halo(m, g, side).wait_recv(), 0, 1)
            kcol = qcol // GROUP * pair + qcol % GROUP
            vcol = kcol + GROUP
            scores = lax.dot_general(
                qbuf[m, :, qcol:qcol + HDIM], kv[m, :, kcol:kcol + HDIM], (((1,), (1,)), ((), ())),
                preferred_element_type=F32,
            )
            scores = jnp.where(allowed, scores, -1e30)
            weights = jnp.exp2((scores - jnp.max(scores, axis=-1, keepdims=True)) * scale)
            total_weight = jnp.sum(weights, axis=-1, keepdims=True)
            head = jnp.dot(weights.astype(BF), kv[m, :, vcol:vcol + HDIM], preferred_element_type=F32)
            mixed[:, qcol:qcol + HDIM] = (head / total_weight).astype(BF)
        for c in range(chunks):
            part, col = c * chunk // heads_width, c * chunk % heads_width
            w = wall[3, :, part * half:(part + 1) * half, col:col + chunk].reshape(heads_width, chunk)
            cols = slice(c * chunk, (c + 1) * chunk)
            projection = jnp.dot(mixed[...], w, preferred_element_type=F32)
            hid[m, :, cols] = (xin[m, :, cols].astype(F32) + valid * projection).astype(BF)

            @pl.when(section < sections - 1)
            def _():
                hop(m, c).start()

        pltpu.make_async_copy(hid.at[m], out.at[0, m], out_sem.at[m]).start()

    def stage(i, _):
        @pl.when(i < micros)
        def _():
            enter(i)
            for slab in range(2):
                for j in range(pairs):
                    keys_values(i, slab, j)

        @pl.when(i > 0)
        def _():
            attend(i - 1)

        @pl.when(i < micros)
        def _():
            queries(i)

        return 0

    lax.fori_loop(0, micros + 1, stage, 0)

    for phase in range(2):
        all_sent(phase)

    @pl.when(section >= 2)
    def _():
        all_sent(2)

    @pl.when(lends)
    def _():
        all_sent(3)
        sent = spread_sent(3)
        pltpu.make_async_copy(sent, sent, lent_send).wait()

    def finish(m, _):
        pltpu.make_async_copy(hid.at[m], out.at[0, m], out_sem.at[m]).wait()
        for g in range(groups):
            each_side(lambda side: halo(m, g, side).wait_send(), 1, 0)

        @pl.when(section < sections - 1)
        def _():
            for c in range(chunks):
                hop(m, c).wait_send()

        return 0

    lax.fori_loop(0, micros, finish, 0)


def on_device(frames, norm_gain, w_qkv, w_out, lengths, windows, shifts):
    micros, rows, width = frames.shape
    depth = w_qkv.shape[1]
    heads_width = w_qkv.shape[2] // 3
    groups = heads_width // GROUP
    tms = lax.axis_size("tm")
    dma = pltpu.SemaphoreType.DMA
    hbm = pl.BlockSpec(memory_space=pltpu.HBM)
    return pl.pallas_call(
        kernel,
        out_shape=jax.ShapeDtypeStruct((1, micros, rows, width), BF),
        in_specs=[hbm] * 7,
        out_specs=hbm,
        scratch_shapes=[
            pltpu.VMEM((4, tms, depth, heads_width), BF),
            pltpu.VMEM((2, tms, depth, LENT), BF),
            pltpu.VMEM((micros, rows, width), BF),
            pltpu.VMEM((micros, rows + 2 * WMAX, 2 * heads_width), BF),
            pltpu.VMEM((rows, width), BF),
            pltpu.VMEM((micros, rows, heads_width), BF),
            pltpu.VMEM((rows, heads_width), BF),
            pltpu.VMEM((micros, rows, width), BF),
            pltpu.VMEM(norm_gain.shape, BF),
            pltpu.SMEM((micros,), jnp.int32),
            pltpu.SMEM(windows.shape, jnp.int32),
            pltpu.SMEM(shifts.shape, jnp.int32),
            dma((2 * groups + 3,)), dma((4,)), dma((4,)), dma((4, 4, tms)), dma((2,)), dma, dma, dma,
            dma((micros, groups, 2)), dma((micros, groups, 2)), dma((micros, 4)), dma((micros, 4)), dma((micros,)),
        ],
        compiler_params=pltpu.CompilerParams(
            collective_id=0, has_side_effects=True, vmem_limit_bytes=60 << 20
        ),
        name="relay",
    )(frames, norm_gain, w_qkv, w_out, lengths.reshape(micros), windows, shifts)


def solution(mesh):
    return jax.shard_map(
        on_device,
        mesh=mesh,
        in_specs=(
            P(None, "tm", None),
            P("section", None),
            P("section", "tm", None),
            P("section", "tm", None),
            P(),
            P(),
            P(),
        ),
        out_specs=P("section", None, "tm", None),
        check_vma=False,
    )
```

```python
import functools
import math

import jax
import jax.numpy as jnp
from jax import lax
from jax.experimental import pallas as pl
from jax.experimental.pallas import tpu as pltpu
from jax.sharding import PartitionSpec as P

HDIM = 128
WMAX = 64
MESH = pl.DeviceIdType.MESH
NY, NZ = 4, 8
STEP = ((0, 1), (0, -1), (1, 0), (-1, 0))
FLIP = (1, 0, 3, 2)
LAG = 6
GROUP = 4 * HDIM
LENT = 3 * HDIM
BF = jnp.bfloat16
F32 = jnp.float32


def spread_trees():
    first, second = {}, {}
    for dz in range(1, NZ):
        first[0, dz] = second[0, dz] = 0 if dz <= 4 else 1
    for dz in range(NZ):
        first[1, dz], first[2, dz], first[3, dz] = 2, 2, 3
    second[1, 0], second[2, 0], second[3, 0] = 2, 2, 3
    for dy in range(1, NY):
        for dz in range(1, NZ):
            second[dy, dz] = 0 if dz <= 4 else 1
    second[1, 4], second[2, 4], second[3, 4], second[2, 5] = 2, 2, 3, 2

    def mirrored(tree):
        return {((-y) % NY, (-z) % NZ): FLIP[d] for (y, z), d in tree.items()}

    return [first, mirrored(first), second, mirrored(second)]


def before(offset, d):
    return ((offset[0] - STEP[d][0]) % NY, (offset[1] - STEP[d][1]) % NZ)


def spread_rounds():
    trees = spread_trees()
    kids = {}
    for part, tree in enumerate(trees):
        for offset, d in tree.items():
            kids.setdefault((part, before(offset, d)), []).append((part, offset))

    def height(node):
        return 1 + max([height(k) for k in kids.get(node, [])], default=0)

    def size(node):
        return 1 + sum(size(k) for k in kids.get(node, []))

    sent = {(part, (0, 0)): -LAG for part in range(4)}
    todo = {(part, offset): d for part, tree in enumerate(trees) for offset, d in tree.items()}
    rounds = []
    while todo:
        row = [None] * 4
        for d in range(4):
            ready = [
                n for n, way in todo.items()
                if way == d and sent.get((n[0], before(n[1], d)), 10**6) + LAG <= len(rounds)
            ]
            if ready:
                row[d] = max(ready, key=lambda n: (height(n), size(n)))
        for d in range(4):
            if row[d] is not None:
                sent[row[d]] = len(rounds)
                del todo[row[d]]
        rounds.append(row)
    return rounds


def kernel(
    frames, gain_hbm, w_qkv, w_out, lengths_hbm, windows_hbm, shifts_hbm, out,
    wall, lent, xin, kv, normed, qbuf, mixed, total, hid, gain, lengths, windows, shifts,
    own_sem, small_sem, spread_send, spread_recv, lend_sem, lent_send, lent_recv, frame_sem, halo_send, halo_recv, hop_send, hop_recv,
    out_sem,
):
    section = lax.axis_index("section")
    sections = lax.axis_size("section")
    tm = lax.axis_index("tm")
    tms = lax.axis_size("tm")
    y, z = tm // NZ, tm % NZ
    micros, rows, width = xin.shape
    heads_width = wall.shape[3]
    groups = heads_width // GROUP
    depth = w_qkv.shape[1]
    quarter, half = depth // 4, depth // 2
    pair = 2 * GROUP
    pairs = heads_width // pair
    scale = math.log2(math.e) / math.sqrt(HDIM)

    def at(dy, dz):
        return ((y + dy + NY) % NY) * NZ + (z + dz + NZ) % NZ

    own = []

    def take(source, target):
        own.append(pltpu.make_async_copy(source, target, own_sem.at[len(own)]))

    for g in range(groups):
        for kind in range(2):
            take(
                w_qkv.at[0, :, pl.ds((1 + kind) * heads_width + g * GROUP, GROUP)],
                wall.at[g // pairs, tm, :, pl.ds(g % pairs * pair + kind * GROUP, GROUP)],
            )
    take(w_qkv.at[0, :, pl.ds(0, heads_width)], wall.at[2, tm])
    for i in range(2):
        take(w_out.at[0, :, pl.ds(i * heads_width, heads_width)], wall.at[3, tm, pl.ds(i * half, half)])
    small = [
        pltpu.make_async_copy(source, target, small_sem.at[i])
        for i, (source, target) in enumerate(
            ((gain_hbm, gain), (lengths_hbm, lengths), (windows_hbm, windows), (shifts_hbm, shifts))
        )
    ]
    for c in own + small:
        c.start()
    frame_copy = pltpu.make_async_copy(frames, xin, frame_sem)

    @pl.when(section == 0)
    def _():
        frame_copy.start()

    barrier = pltpu.get_barrier_semaphore()
    for dy, dz in STEP:
        pl.semaphore_signal(barrier, inc=1, device_id=(section, at(dy, dz)), device_id_type=MESH)
    for d in (1, -1):
        pl.semaphore_signal(barrier, inc=1, device_id=(section, (tm + d + tms) % tms), device_id_type=MESH)
    for d in (1, -1, 2, -2):
        pl.semaphore_signal(
            barrier, inc=1, device_id=((section + d + sections) % sections, tm), device_id_type=MESH
        )

    @pl.when(tm == 0)
    def _():
        for m in range(micros):
            kv[m, :WMAX, :] = jnp.zeros((WMAX, 2 * heads_width), BF)

    @pl.when(tm == tms - 1)
    def _():
        for m in range(micros):
            kv[m, WMAX + rows:, :] = jnp.zeros((WMAX, 2 * heads_width), BF)

    borrows, lends = section < 2, section >= sections - 2

    for c in small + own:
        c.wait()
    pl.semaphore_wait(barrier, 10)

    @pl.when(section == 0)
    def _():
        frame_copy.wait()

    window = windows[section]
    shift = shifts[section]

    def window_of(pos):
        n = pos - shift
        guess = jnp.floor((n.astype(F32) + 0.5) / window.astype(F32)).astype(jnp.int32)
        rest = n - guess * window
        return guess + (rest >= window).astype(jnp.int32) - (rest < 0).astype(jnp.int32)

    query_pos = tm * rows + lax.broadcasted_iota(jnp.int32, (rows, 1), 0)
    key_pos = tm * rows - WMAX + lax.broadcasted_iota(jnp.int32, (1, rows + 2 * WMAX), 1)
    same = query_pos == key_pos

    def halo(m, g, side):
        src = (rows, WMAX)[side]
        dst = (0, WMAX + rows)[side]
        return pltpu.make_async_remote_copy(
            src_ref=kv.at[m, pl.ds(src, WMAX), pl.ds(g * pair, pair)],
            dst_ref=kv.at[m, pl.ds(dst, WMAX), pl.ds(g * pair, pair)],
            send_sem=halo_send.at[m, g, side], recv_sem=halo_recv.at[m, g, side],
            device_id=(section, (tm + (1, -1)[side] + tms) % tms), device_id_type=MESH,
        )

    def each_side(act, before_me, after_me):
        @pl.when(tm < tms - 1)
        def _():
            act(after_me)

        @pl.when(tm > 0)
        def _():
            act(before_me)

    chunk = heads_width // 2
    chunks = width // chunk

    def hop(m, c):
        return pltpu.make_async_remote_copy(
            src_ref=hid.at[m, :, pl.ds(c * chunk, chunk)], dst_ref=xin.at[m, :, pl.ds(c * chunk, chunk)],
            send_sem=hop_send.at[m, c], recv_sem=hop_recv.at[m, c],
            device_id=((section + 1) % sections, tm), device_id_type=MESH,
        )

    def project(slab, col):
        w = wall[slab, :, :, col:col + pair].reshape(width, pair)
        return jnp.dot(normed[...], w, preferred_element_type=F32).astype(BF)

    def enter(m):
        @pl.when(section > 0)
        def _():
            for c in range(chunks):
                hop(m, c).wait_recv()

        x = xin[m].astype(F32)
        centered = x - jnp.mean(x, axis=-1, keepdims=True)
        variance = jnp.mean(centered * centered, axis=-1, keepdims=True)
        normed[...] = (centered * lax.rsqrt(variance + 1e-05) * gain[...].astype(F32)).astype(BF)

    def keys_values(m, slab, i):
        g = slab * pairs + i
        cols = pl.ds(pl.multiple_of(g * pair, pair), pair)
        kv[m, pl.ds(WMAX, rows), cols] = project(slab, i * pair)
        each_side(lambda side: halo(m, g, side).start(), 1, 0)

    rounds = spread_rounds()
    near_cols = heads_width - LENT
    lent_cols = pl.ds(near_cols, LENT)

    def blocks(phase, source, first, count):
        line = pl.ds(first, count)
        if phase == 0:
            return wall.at[pl.ds(0, 2), source, line]
        if phase == 1:
            return wall.at[pl.ds(2, 2), source, line, pl.ds(0, near_cols)]
        if phase == 2:
            return wall.at[pl.ds(2, 2), source, line, lent_cols]
        return lent.at[:, source, line]

    def slot(phase, part, offset):
        return blocks(phase, at(-offset[0], -offset[1]), part * quarter, quarter)

    def spread_copy(phase, part, offset, d):
        block = slot(phase, part, offset)
        return pltpu.make_async_remote_copy(
            src_ref=block, dst_ref=block, send_sem=spread_send.at[phase],
            recv_sem=spread_recv.at[phase, part, ((offset[0] + STEP[d][0]) % NY) * NZ + (offset[1] + STEP[d][1]) % NZ],
            device_id=(section, at(*STEP[d])), device_id_type=MESH,
        )

    def lend():
        return pltpu.make_async_remote_copy(
            src_ref=blocks(2, tm, 0, depth), dst_ref=blocks(3, tm, 0, depth), send_sem=lend_sem.at[0],
            recv_sem=lend_sem.at[1], device_id=((section + sections - 2) % sections, tm), device_id_type=MESH,
        )

    def spread_arrived(phase, part, offset):
        block = slot(phase, part, offset)
        pltpu.make_async_copy(block, block, spread_recv.at[phase, part, offset[0] * NZ + offset[1]]).wait()
        if phase == 3:
            pltpu.make_async_remote_copy(
                src_ref=block, dst_ref=slot(2, part, offset), send_sem=lent_send, recv_sem=lent_recv,
                device_id=((section + 2) % sections, tm), device_id_type=MESH,
            ).start()

    def spread(phase, behind=()):
        seen = {(part, (0, 0)) for part in range(4)}
        for r, row in enumerate(rounds):
            if r == LAG:
                for node in behind:
                    spread_arrived(*node)
            for d, node in enumerate(row):
                if node is None:
                    continue
                part, source = node[0], before(node[1], d)
                if (part, source) not in seen:
                    spread_arrived(phase, part, source)
                    seen.add((part, source))
                spread_copy(phase, part, source, d).start()
        every = [(part, (o // NZ, o % NZ)) for part in range(4) for o in range(1, NY * NZ)]
        return [(phase, *node) for node in every if node not in seen]

    def spread_sent(phase):
        if phase == 3:
            sent = lent.at[:, pl.ds(0, NY * NZ - 1)]
        elif phase == 0:
            sent = wall.at[pl.ds(0, 2), pl.ds(0, NY * NZ - 1)]
        else:
            sent = wall.at[pl.ds(2, 2), pl.ds(0, NY * NZ - 1), :, pl.ds(0, near_cols) if phase == 1 else lent_cols]
        return sent

    def all_sent(phase):
        sent = spread_sent(phase)
        pltpu.make_async_copy(sent, sent, spread_send.at[phase]).wait()

    @pl.when(borrows)
    def _():
        lend().start()

    @pl.when(lends)
    def _():
        lend().wait_recv()
        for node in spread(3):
            spread_arrived(*node)

    for node in spread(1, spread(0)):
        spread_arrived(*node)

    @pl.when(borrows)
    def _():
        lend().wait_send()
        sent = spread_sent(2)
        pltpu.make_async_copy(sent, sent, lent_recv).wait()

    @pl.when(section >= 2)
    def _():
        for node in spread(2):
            spread_arrived(*node)

    def queries(m):
        for col in range(0, heads_width, pair):
            qbuf[m, :, col:col + pair] = project(2, col)

    def attend(m):
        length = lengths[m]
        near = (window_of(query_pos) == window_of(key_pos)) & (key_pos >= 0) & (key_pos < rows * tms)
        allowed = near & ((key_pos < length) | same)
        valid = (query_pos < length).astype(F32)
        mid = heads_width // 2
        for first in (0, mid):
            for g in range(first // GROUP, (first + mid) // GROUP):
                each_side(lambda side: halo(m, g, side).wait_recv(), 0, 1)
            for qcol in range(first, first + mid, HDIM):
                kcol = qcol // GROUP * pair + qcol % GROUP
                vcol = kcol + GROUP
                scores = lax.dot_general(
                    qbuf[m, :, qcol:qcol + HDIM], kv[m, :, kcol:kcol + HDIM], (((1,), (1,)), ((), ())),
                    preferred_element_type=F32,
                )
                scores = jnp.where(allowed, scores, -1e30)
                weights = jnp.exp2((scores - jnp.max(scores, axis=-1, keepdims=True)) * scale)
                total_weight = jnp.sum(weights, axis=-1, keepdims=True)
                head = jnp.dot(weights.astype(BF), kv[m, :, vcol:vcol + HDIM], preferred_element_type=F32)
                mixed[:, qcol:qcol + HDIM] = (head / total_weight).astype(BF)
            for c in range(chunks):
                part, col = c * chunk // heads_width, c * chunk % heads_width
                w = wall[3, first // half:(first + mid) // half, part * half:(part + 1) * half, col:col + chunk]
                cols = slice(c * chunk, (c + 1) * chunk)
                projection = jnp.dot(mixed[:, first:first + mid], w.reshape(mid, chunk), preferred_element_type=F32)
                if first == 0:
                    total[:, cols] = projection
                    continue
                projection = total[:, cols] + projection
                hid[m, :, cols] = (xin[m, :, cols].astype(F32) + valid * projection).astype(BF)

                @pl.when(section < sections - 1)
                def _():
                    hop(m, c).start()

        pltpu.make_async_copy(hid.at[m], out.at[0, m], out_sem.at[m]).start()

    def stage(i, _):
        @pl.when(i < micros)
        def _():
            enter(i)
            for slab in range(2):
                for j in range(pairs):
                    keys_values(i, slab, j)

        @pl.when(i > 0)
        def _():
            attend(i - 1)

        @pl.when(i < micros)
        def _():
            queries(i)

        return 0

    lax.fori_loop(0, micros + 1, stage, 0)

    for phase in range(2):
        all_sent(phase)

    @pl.when(section >= 2)
    def _():
        all_sent(2)

    @pl.when(lends)
    def _():
        all_sent(3)
        sent = spread_sent(3)
        pltpu.make_async_copy(sent, sent, lent_send).wait()

    def finish(m, _):
        pltpu.make_async_copy(hid.at[m], out.at[0, m], out_sem.at[m]).wait()
        for g in range(groups):
            each_side(lambda side: halo(m, g, side).wait_send(), 1, 0)

        @pl.when(section < sections - 1)
        def _():
            for c in range(chunks):
                hop(m, c).wait_send()

        return 0

    lax.fori_loop(0, micros, finish, 0)


def on_device(frames, norm_gain, w_qkv, w_out, lengths, windows, shifts):
    micros, rows, width = frames.shape
    depth = w_qkv.shape[1]
    heads_width = w_qkv.shape[2] // 3
    groups = heads_width // GROUP
    tms = lax.axis_size("tm")
    dma = pltpu.SemaphoreType.DMA
    hbm = pl.BlockSpec(memory_space=pltpu.HBM)
    return pl.pallas_call(
        kernel,
        out_shape=jax.ShapeDtypeStruct((1, micros, rows, width), BF),
        in_specs=[hbm] * 7,
        out_specs=hbm,
        scratch_shapes=[
            pltpu.VMEM((4, tms, depth, heads_width), BF),
            pltpu.VMEM((2, tms, depth, LENT), BF),
            pltpu.VMEM((micros, rows, width), BF),
            pltpu.VMEM((micros, rows + 2 * WMAX, 2 * heads_width), BF),
            pltpu.VMEM((rows, width), BF),
            pltpu.VMEM((micros, rows, heads_width), BF),
            pltpu.VMEM((rows, heads_width), BF),
            pltpu.VMEM((rows, width), F32),
            pltpu.VMEM((micros, rows, width), BF),
            pltpu.VMEM(norm_gain.shape, BF),
            pltpu.SMEM((micros,), jnp.int32),
            pltpu.SMEM(windows.shape, jnp.int32),
            pltpu.SMEM(shifts.shape, jnp.int32),
            dma((2 * groups + 3,)), dma((4,)), dma((4,)), dma((4, 4, tms)), dma((2,)), dma, dma, dma,
            dma((micros, groups, 2)), dma((micros, groups, 2)), dma((micros, 4)), dma((micros, 4)), dma((micros,)),
        ],
        compiler_params=pltpu.CompilerParams(
            collective_id=0, has_side_effects=True, vmem_limit_bytes=60 << 20
        ),
        name="relay",
    )(frames, norm_gain, w_qkv, w_out, lengths.reshape(micros), windows, shifts)


def solution(mesh):
    return jax.shard_map(
        on_device,
        mesh=mesh,
        in_specs=(
            P(None, "tm", None),
            P("section", None),
            P("section", "tm", None),
            P("section", "tm", None),
            P(),
            P(),
            P(),
        ),
        out_specs=P("section", None, "tm", None),
        check_vma=False,
    )
```
